32 devices in a mesh: row: 8 (over y, x, core), col: 4 (over z).
Axes of the slice: x: 2, y: 2, z: 4, core: 2. Of those that a mesh axis runs over, the one named last changes fastest.
Arguments:
- amplitudes: bfloat16 [2, 2048, 2048], P(None, 'row', 'col'), may hold values from -6 to 6
- factor: bfloat16 [2048, 4096], P('row', 'col'), may hold values from -0.125 to 0.125
- kernel: float32 [4096, 4096], P('row', 'col'), may hold values from -6 to 6
Outputs:
- ladder: bfloat16 [2, 2048, 2048], P(None, 'row', 'col')
The draws below stay inside these ranges and needn't reach their ends.
All inputs are finite; a program needn't handle non-finite values.
Results may differ from the reference program's by a relative error of at most 0.015.
Values may be sent and summed in bfloat16 or wider, within the bound.
No kernel may reach another device: no remote copies, remote signals or barrier semaphores. Data moves between devices by JAX's collectives and lax.ppermute only.
A program may use at most 64 MiB of HBM per device.

```python
import jax
import jax.numpy as jnp
from jax import lax

V = 2048
G = 4096
PAIRS = 2
GRID_COL = 1024


def steps_of(key, shape, pieces, least, high):
    factor_of = 1.0
    for dim, blocks in pieces:
        steps = jax.random.uniform(jax.random.fold_in(jax.random.fold_in(key, 6), dim), (blocks,), jnp.float32, least / len(pieces), high / len(pieces))
        factor_of = factor_of * jnp.repeat(jnp.exp(steps), shape[dim] // blocks).reshape((-1,) + (1,) * (len(shape) - 1 - dim))
    return factor_of


def gaussian(key, dims, deviation, most, pieces=(), kind=jnp.bfloat16):
    entries = jax.random.normal(key, dims, jnp.float32) * deviation
    if len(pieces) > 0:
        entries = steps_of(key, dims, pieces, -0.22, 0.18) * entries
    return jnp.clip(entries, min=-most, max=most).astype(kind)


def setup_inputs(seed: int = 0) -> dict:
    splits = jax.random.split(jax.random.key(seed), 4)
    amplitudes = gaussian(splits[0], (PAIRS, V, V), 1.0, 6.0, ((1, 8), (2, 4)))
    factor = gaussian(splits[1], (V, G), V ** -0.5, 0.125, ((0, 8), (1, 4)))
    kernel = gaussian(splits[2], (G, G), 1.0, 6.0, ((0, 8), (1, 4)), jnp.float32)
    return {"amplitudes": amplitudes, "factor": factor, "kernel": kernel}


def reference(amplitudes, factor, kernel):
    block_count = G // GRID_COL

    def single_pair(amplitude_pair):
        projected = jnp.dot(amplitude_pair, factor, preferred_element_type=jnp.float32).astype(jnp.bfloat16)
        grid_pairs = jnp.dot(factor.T, projected, preferred_element_type=jnp.float32)
        scaled = (kernel * grid_pairs).astype(jnp.bfloat16)

        def add_block(running, block):
            start = (block * GRID_COL).astype(jnp.int32)
            scaled_part = lax.dynamic_slice_in_dim(scaled, start, GRID_COL, 1)
            factor_part = lax.dynamic_slice_in_dim(factor, start, GRID_COL, 1)
            term = jnp.dot(scaled_part, factor_part.T, preferred_element_type=jnp.float32).astype(jnp.bfloat16)
            term = lax.optimization_barrier(term)
            return running + term.astype(jnp.float32), None

        zeroed = jnp.zeros((G, V), jnp.float32)
        half_back, _ = lax.scan(add_block, zeroed, jnp.arange(block_count, dtype=jnp.int32))
        half_back = half_back.astype(jnp.bfloat16)
        return jnp.dot(factor, half_back, preferred_element_type=jnp.float32).astype(jnp.bfloat16)

    return lax.map(single_pair, amplitudes)
```

```python
import functools

import jax
import jax.numpy as jnp
from jax import lax
from jax.experimental import pallas as pl
from jax.experimental.pallas import tpu as pltpu
from jax.sharding import PartitionSpec as P

BF16 = jnp.bfloat16
F32 = jnp.float32
ANY = pl.BlockSpec(memory_space=pltpu.HBM)


def flipped(value, bits):
    total = 0
    for t in range(bits):
        total = total + (((value >> t) & 1) << (bits - 1 - t))
    return total


def params(vmem):
    return pltpu.CompilerParams(vmem_limit_bytes=vmem)


def where_am_i(bits):
    row, col = lax.axis_index("row"), lax.axis_index("col")
    core, chip = lax.rem(row, 2), row // 2
    offset = chip ^ col
    base = jnp.where(core == 0, offset, flipped(offset, bits))
    return core, base


def copy_all(pairs, sems):
    copies = [pltpu.make_async_copy(a, b, sems.at[s]) for s, (a, b) in enumerate(pairs)]
    for copy in copies:
        copy.start()
    return copies


def plane_pairs(own, other, room, core, rows, bits):
    pairs = []
    for j, ref in enumerate(own):
        pairs.append((ref, room.at[pl.ds((2 * j + core) * rows, rows)]))
    for j, ref in enumerate(other):
        pairs.append((ref, room.at[pl.ds((2 * flipped(j, bits) + 1 - core) * rows, rows)]))
    return pairs


def project_kernel(bits, *refs):
    n = 1 << bits
    terms, own, other = refs[:n], refs[n : 2 * n], refs[2 * n : 3 * n]
    out, held, room, total, sems = refs[3 * n :]
    core, base = where_am_i(bits)
    rows, width = own[0].shape
    depth = terms[0].shape[1]
    pairs = [(terms[l], held.at[l]) for l in range(n)] + plane_pairs(own, other, room, core, rows, bits)
    for copy in copy_all(pairs, sems):
        copy.wait()
    tile = min(width, 512)

    @pl.loop(0, width // tile)
    def _(step):
        at = pl.ds(pl.multiple_of(step * tile, tile), tile)
        acc = jnp.zeros((out.shape[0], tile), F32)
        for l in range(n):
            start = pl.multiple_of((base ^ l) * depth, depth)
            acc = acc + jnp.dot(held[l], room[pl.ds(start, depth), at], preferred_element_type=F32)
        total[:, at] = acc.astype(BF16)

    copy = pltpu.make_async_copy(total, out, sems.at[0])
    copy.start()
    copy.wait()


def project(terms, own, other, bits):
    n = len(terms)
    m, depth = terms[0].shape
    rows, width = own[0].shape
    return pl.pallas_call(
        functools.partial(project_kernel, bits),
        out_shape=jax.ShapeDtypeStruct((m, width), BF16),
        in_specs=[ANY] * (3 * n),
        out_specs=ANY,
        scratch_shapes=[
            pltpu.VMEM((n, m, depth), BF16),
            pltpu.VMEM((2 * n * rows, width), BF16),
            pltpu.VMEM((m, width), BF16),
            pltpu.SemaphoreType.DMA((3 * n,)),
        ],
        compiler_params=params(32 << 20),
        cost_estimate=pl.CostEstimate(flops=2 * m * n * depth * width, bytes_accessed=2 * n * (m * depth + 2 * rows * width), transcendentals=0),
        name="project",
    )(*terms, *own, *other)


def grid_kernel(bits, *refs):
    n = 1 << bits
    first, second = refs[:n], refs[n : 2 * n]
    own, other = refs[2 * n : 3 * n], refs[3 * n : 4 * n]
    kernel_own, kernel_other = refs[4 * n : 4 * n + 2]
    outs = refs[4 * n + 2 : 6 * n + 2]
    proj, room, coulomb, scaled, back, sems, out_sems = refs[6 * n + 2 :]
    core, _ = where_am_i(bits)
    rows, width = own[0].shape
    half = kernel_own.shape[0]
    pairs = []
    for j in range(n):
        pairs.append((own[j], room.at[pl.ds(2 * j * rows, rows)]))
        pairs.append((other[flipped(j, bits)], room.at[pl.ds((2 * j + 1) * rows, rows)]))
        pairs.append((first[j], proj.at[pl.ds(2 * j * rows, rows)]))
        pairs.append((second[j], proj.at[pl.ds((2 * j + 1) * rows, rows)]))
    pairs.append((kernel_own, coulomb.at[pl.ds(core * half, half)]))
    pairs.append((kernel_other, coulomb.at[pl.ds((1 - core) * half, half)]))
    for copy in copy_all(pairs, sems):
        copy.wait()
    tile = min(proj.shape[1], 256)

    @pl.loop(0, proj.shape[1] // tile)
    def _(step):
        at = pl.ds(pl.multiple_of(step * tile, tile), tile)
        grid = lax.dot_general(room[...], proj[:, at], (((0,), (0,)), ((), ())), preferred_element_type=F32)
        scaled[:, at] = (coulomb[:, at] * grid).astype(BF16)

    copies = []
    for h in (1, 0):
        for j in range(n - 1, -1, -1):
            at = pl.ds((2 * j + h) * rows, rows)
            back[at, :] = jnp.dot(room[at, :], scaled[...], preferred_element_type=F32).astype(BF16)
            copy = pltpu.make_async_copy(back.at[at], outs[h * n + j], out_sems.at[h * n + j])
            copy.start()
            copies.append(copy)
    for copy in copies:
        copy.wait()


def grid(first, second, own, other, kernel_own, kernel_other, bits):
    n = len(first)
    rows, width = own[0].shape
    cols = first[0].shape[1]
    outs = pl.pallas_call(
        functools.partial(grid_kernel, bits),
        out_shape=[jax.ShapeDtypeStruct((rows, cols), BF16)] * (2 * n),
        in_specs=[ANY] * (4 * n + 2),
        out_specs=[ANY] * (2 * n),
        scratch_shapes=[
            pltpu.VMEM((2 * n * rows, cols), BF16),
            pltpu.VMEM((2 * n * rows, width), BF16),
            pltpu.VMEM((width, cols), F32),
            pltpu.VMEM((width, cols), BF16),
            pltpu.VMEM((2 * n * rows, cols), BF16),
            pltpu.SemaphoreType.DMA((4 * n + 2,)),
            pltpu.SemaphoreType.DMA((2 * n,)),
        ],
        compiler_params=params(48 << 20),
        cost_estimate=pl.CostEstimate(flops=8 * n * rows * width * cols, bytes_accessed=12 * n * rows * cols + 4 * width * cols, transcendentals=0),
        name="grid",
    )(*first, *second, *own, *other, kernel_own, kernel_other)
    return list(outs[:n]), list(outs[n:])


def back_kernel(bits, *refs):
    n = 1 << bits
    q = bits + 1
    parts, own, other = refs[:q], refs[q : q + n], refs[q + n : q + 2 * n]
    outs = refs[q + 2 * n : q + 3 * n]
    given, room, results, sems, out_sems = refs[q + 3 * n :]
    core, base = where_am_i(bits)
    rows, width = own[0].shape
    depth = outs[0].shape[1]
    pairs = [(parts[i], given.at[i]) for i in range(q)] + plane_pairs(own, other, room, core, rows, bits)
    for copy in copy_all(pairs, sems):
        copy.wait()
    left = total([given[i] for i in range(q)])
    copies = []
    for l in range(n - 1, -1, -1):
        right = room[pl.ds(pl.multiple_of((base ^ l) * depth, depth), depth), :]
        results[l] = lax.dot_general(left, right, (((1,), (1,)), ((), ())), preferred_element_type=F32).astype(BF16)
        copy = pltpu.make_async_copy(results.at[l], outs[l], out_sems.at[l])
        copy.start()
        copies.append(copy)
    for copy in copies:
        copy.wait()


def back(parts, own, other, bits):
    n, q = len(own), len(parts)
    rows, width = own[0].shape
    m, depth = parts[0].shape[0], 2 * rows
    outs = pl.pallas_call(
        functools.partial(back_kernel, bits),
        out_shape=[jax.ShapeDtypeStruct((m, depth), BF16)] * n,
        in_specs=[ANY] * (q + 2 * n),
        out_specs=[ANY] * n,
        scratch_shapes=[
            pltpu.VMEM((q, m, width), BF16),
            pltpu.VMEM((2 * n * rows, width), BF16),
            pltpu.VMEM((n, m, depth), BF16),
            pltpu.SemaphoreType.DMA((q + 2 * n,)),
            pltpu.SemaphoreType.DMA((n,)),
        ],
        compiler_params=params(32 << 20),
        cost_estimate=pl.CostEstimate(flops=2 * m * n * depth * width, bytes_accessed=2 * n * (m * depth + 2 * rows * width), transcendentals=0),
        name="back",
    )(*parts, *own, *other)
    return list(outs)


def pick_kernel(bits, *refs):
    n = 1 << bits
    blocks, outs, (room, sems) = refs[:n], refs[n : 2 * n], refs[2 * n :]
    _, base = where_am_i(bits)
    for copy in copy_all([(blocks[l], room.at[l]) for l in range(n)], sems):
        copy.wait()
    for copy in copy_all([(room.at[base ^ j], outs[j]) for j in range(n)], sems):
        copy.wait()


def pick(blocks, bits):
    n = len(blocks)
    return pl.pallas_call(
        functools.partial(pick_kernel, bits),
        out_shape=[jax.ShapeDtypeStruct(blocks[0].shape, BF16)] * n,
        in_specs=[ANY] * n,
        out_specs=[ANY] * n,
        scratch_shapes=[pltpu.VMEM((n, *blocks[0].shape), BF16), pltpu.SemaphoreType.DMA((n,))],
        compiler_params=params(16 << 20),
        cost_estimate=pl.CostEstimate(flops=0, bytes_accessed=4 * n * blocks[0].size, transcendentals=0),
        name="pick",
    )(*blocks)


def total(parts):
    return sum(part.astype(F32) for part in parts).astype(BF16)


def after(value, *others):
    return lax.optimization_barrier((value, *others))[0]


def per_device(rows, cols, amplitudes, factor, kernel):
    chips = rows // 2
    bits = chips.bit_length() - 1
    core = lax.rem(lax.axis_index("row"), 2)

    def bit_of(step, row):
        return step if row % 2 == 0 else bits - 1 - step

    def swap(value):
        return lax.ppermute(value, "row", [(r, r ^ 1) for r in range(rows)])

    def to_plane(mask):
        def send(value):
            return lax.ppermute(value, "row", [(r, r ^ (2 * (mask if r % 2 == 0 else flipped(mask, bits)))) for r in range(rows)])

        return send

    def to_line(step):
        def send(value):
            pairs = []
            for r in range(rows):
                for c in range(cols):
                    pairs.append((r * cols + c, r * cols + (c ^ (1 << bit_of(step, r)))))
            return lax.ppermute(value, ("row", "col"), pairs)

        return send

    plane = [to_plane(1 << t) for t in range(bits)]
    line = [to_line(t) for t in range(bits)]

    def gather(block, sends, gates=()):
        blocks = [block]
        for t, send in enumerate(sends):
            first = after(block, gates[t]) if t < len(gates) else block
            blocks = blocks + [send(b) for b in [first] + blocks[1:]]
        return blocks

    def scatter(blocks, sends, gate=None):
        parts, marks = [], []
        for t in range(len(sends) - 1, -1, -1):
            n = 1 << t
            away = blocks[n:]
            if gate is not None and not marks:
                away = [after(block, gate) for block in away]
            got = [sends[t](block) for block in away]
            marks.append(got[-1])
            parts.append(got[0])
            blocks = [blocks[0]] + [total([blocks[j], got[j]]) for j in range(1, n)]
        return [blocks[0], *parts], marks[0]

    middle = 1 << (bits - 1)
    mine = lax.dynamic_index_in_dim(amplitudes, core, 0, keepdims=False)
    theirs = lax.dynamic_index_in_dim(amplitudes, 1 - core, 0, keepdims=False)

    line_own = gather(factor, line)
    cols_own = gather(factor, plane)
    kernel_other = swap(kernel)
    second = swap(theirs)
    cols_other = [swap(b) for b in cols_own]
    terms0 = gather(mine, line, [line_own[middle], line_own[-1]])
    terms1 = gather(second, line, [terms0[middle], terms0[-1]])

    pieces = pick(line_own, bits)
    first_own = [pieces[0]] + [to_plane(j)(pieces[j]) for j in range(1, chips)]
    first_other = [swap(b) for b in first_own]

    proj0 = gather(project(terms0, cols_own, cols_other, bits), plane)
    proj1 = gather(project(terms1, cols_own, cols_other, bits), plane)

    z0, z1 = grid(proj0, proj1, first_own, first_other, kernel, kernel_other, bits)
    s1, mark = scatter(z1, plane)
    s0, _ = scatter(z0, plane, mark)
    o1 = back(s1, cols_own, cols_other, bits)
    o0 = back(s0, cols_own, cols_other, bits)
    t1, mark = scatter(o1, line)
    t0, _ = scatter(o0, line, mark)

    away = swap(total(t1))
    here = total(t0)
    return jnp.where(core == 0, jnp.stack([here, away]), jnp.stack([away, here]))


def solution(mesh):
    placed = (P(None, "row", "col"), P("row", "col"), P("row", "col"))
    rows, cols = mesh.shape["row"], mesh.shape["col"]
    return jax.shard_map(
        functools.partial(per_device, rows, cols), mesh=mesh, in_specs=placed, out_specs=P(None, "row", "col"), check_vma=False
    )
```

```python
import functools

import jax
import jax.numpy as jnp
from jax import lax
from jax.experimental import pallas as pl
from jax.experimental.pallas import tpu as pltpu
from jax.sharding import PartitionSpec as P

BF16 = jnp.bfloat16
F32 = jnp.float32
ANY = pl.BlockSpec(memory_space=pl.ANY)
HBM = pl.BlockSpec(memory_space=pltpu.HBM)


def flipped(value, bits):
    total = 0
    for t in range(bits):
        total = total + (((value >> t) & 1) << (bits - 1 - t))
    return total


def params(vmem):
    return pltpu.CompilerParams(vmem_limit_bytes=vmem)


def where_am_i(bits):
    row, col = lax.axis_index("row"), lax.axis_index("col")
    core, chip = lax.rem(row, 2), row // 2
    offset = chip ^ col
    base = jnp.where(core == 0, offset, flipped(offset, bits))
    return core, base


def copy_all(pairs, sems):
    copies = [pltpu.make_async_copy(a, b, sems.at[s]) for s, (a, b) in enumerate(pairs)]
    for copy in copies:
        copy.start()
    return copies


def plane_pairs(own, other, room, core, rows, bits):
    pairs = []
    for j, ref in enumerate(own):
        pairs.append((ref, room.at[pl.ds((2 * j + core) * rows, rows)]))
    for j, ref in enumerate(other):
        pairs.append((ref, room.at[pl.ds((2 * flipped(j, bits) + 1 - core) * rows, rows)]))
    return pairs


def halves(ref, core):
    half = ref.shape[1] // 2
    return [ref.at[:, pl.ds(pl.multiple_of(which * half, half), half)] for which in (core, 1 - core)]


def project_kernel(bits, *refs):
    n = 1 << bits
    terms, own, other = refs[:n], refs[n : 2 * n], refs[2 * n : 3 * n]
    keep, away, held, room, result, sems = refs[3 * n :]
    core, base = where_am_i(bits)
    rows, width = own[0].shape
    depth = terms[0].shape[1]
    pairs = plane_pairs(own, other, room, core, rows, bits) + [(terms[l], held.at[l]) for l in range(n)]
    for copy in copy_all(pairs, sems):
        copy.wait()
    tile = min(width // 2, 512)

    @pl.loop(0, width // tile)
    def _(step):
        at = pl.ds(pl.multiple_of(step * tile, tile), tile)
        acc = jnp.zeros((rows, tile), F32)
        for l in range(n):
            start = pl.multiple_of((base ^ l) * depth, depth)
            acc = acc + jnp.dot(held[l], room[pl.ds(start, depth), at], preferred_element_type=F32)
        result[:, at] = acc.astype(BF16)

    for copy in copy_all(list(zip(halves(result, core), (keep, away))), sems):
        copy.wait()


def project(terms, own, other, bits):
    n = len(terms)
    m, depth = terms[0].shape
    rows, width = own[0].shape
    return pl.pallas_call(
        functools.partial(project_kernel, bits),
        out_shape=[jax.ShapeDtypeStruct((m, width // 2), BF16)] * 2,
        in_specs=[HBM] * (3 * n),
        out_specs=[ANY] * 2,
        scratch_shapes=[
            pltpu.VMEM((n, m, depth), BF16),
            pltpu.VMEM((2 * n * rows, width), BF16),
            pltpu.VMEM((m, width), BF16),
            pltpu.SemaphoreType.DMA((3 * n,)),
        ],
        compiler_params=params(32 << 20),
        cost_estimate=pl.CostEstimate(flops=1, bytes_accessed=1, transcendentals=0),
        name="project",
    )(*terms, *own, *other)


def grid_kernel(bits, *refs):
    n = 1 << bits
    proj_in, own, other = refs[:n], refs[n : 2 * n], refs[2 * n : 3 * n]
    kernel_own, kernel_other = refs[3 * n : 3 * n + 2]
    outs = refs[3 * n + 2 : 4 * n + 2]
    proj, room, coulomb, scaled, result, sems, tile_sems, out_sems = refs[4 * n + 2 :]
    core, _ = where_am_i(bits)
    rows = own[0].shape[0]
    half = kernel_own.shape[0]
    pairs = []
    for j in range(n):
        pairs.append((own[j], room.at[pl.ds(2 * j * rows, rows)]))
        pairs.append((other[flipped(j, bits)], room.at[pl.ds((2 * j + 1) * rows, rows)]))
        pairs.append((proj_in[j], proj.at[pl.ds(2 * j * rows, 2 * rows)]))
    loads = copy_all(pairs, sems)
    late = copy_all([(kernel_own, coulomb.at[pl.ds(core * half, half)]), (kernel_other, coulomb.at[pl.ds((1 - core) * half, half)])], tile_sems)
    for copy in loads:
        copy.wait()
    for copy in late:
        copy.wait()
    tile = min(proj.shape[1], 256)

    @pl.loop(0, proj.shape[1] // tile)
    def _(step):
        at = pl.ds(pl.multiple_of(step * tile, tile), tile)
        grid = lax.dot_general(room[...], proj[:, at], (((0,), (0,)), ((), ())), preferred_element_type=F32)
        scaled[:, at] = (coulomb[:, at] * grid).astype(BF16)

    copies = []
    for j in range(n - 1, -1, -1):
        at = pl.ds(2 * j * rows, 2 * rows)
        result[at, :] = jnp.dot(room[at, :], scaled[...], preferred_element_type=F32).astype(BF16)
        copy = pltpu.make_async_copy(result.at[at], outs[j], out_sems.at[j])
        copy.start()
        copies.append(copy)
    for copy in copies:
        copy.wait()


def grid(proj, own, other, kernel_own, kernel_other, bits):
    n = len(proj)
    rows, width = own[0].shape
    cols = proj[0].shape[1]
    outs = pl.pallas_call(
        functools.partial(grid_kernel, bits),
        out_shape=[jax.ShapeDtypeStruct((2 * rows, cols), BF16)] * n,
        in_specs=[HBM] * (3 * n) + [ANY] * 2,
        out_specs=[ANY] * n,
        scratch_shapes=[
            pltpu.VMEM((2 * n * rows, cols), BF16),
            pltpu.VMEM((2 * n * rows, width), BF16),
            pltpu.VMEM((width, cols), F32),
            pltpu.VMEM((width, cols), BF16),
            pltpu.VMEM((2 * n * rows, cols), BF16),
            pltpu.SemaphoreType.DMA((3 * n,)),
            pltpu.SemaphoreType.DMA((2,)),
            pltpu.SemaphoreType.DMA((n,)),
        ],
        compiler_params=params(40 << 20),
        cost_estimate=pl.CostEstimate(flops=1, bytes_accessed=1, transcendentals=0),
        name="grid",
    )(*proj, *own, *other, kernel_own, kernel_other)
    return list(outs)


def back_kernel(bits, *refs):
    n = 1 << bits
    keep, came, own, other = refs[0], refs[1], refs[2 : 2 + n], refs[2 + n : 2 + 2 * n]
    outs = refs[2 + 2 * n : 2 + 3 * n]
    given, room, results, sems, out_sems = refs[2 + 3 * n :]
    core, base = where_am_i(bits)
    rows, width = own[0].shape
    depth = outs[0].shape[1]
    pairs = plane_pairs(own, other, room, core, rows, bits) + list(zip((keep, came), halves(given, core)))
    for copy in copy_all(pairs, sems):
        copy.wait()
    copies = []
    for l in range(n - 1, -1, -1):
        right = room[pl.ds(pl.multiple_of((base ^ l) * depth, depth), depth), :]
        results[l] = lax.dot_general(given[...], right, (((1,), (1,)), ((), ())), preferred_element_type=F32).astype(BF16)
        copy = pltpu.make_async_copy(results.at[l], outs[l], out_sems.at[l])
        copy.start()
        copies.append(copy)
    for copy in copies:
        copy.wait()


def back(keep, came, own, other, bits):
    n = len(own)
    rows, width = own[0].shape
    m, depth = keep.shape[0], 2 * rows
    outs = pl.pallas_call(
        functools.partial(back_kernel, bits),
        out_shape=[jax.ShapeDtypeStruct((m, depth), BF16)] * n,
        in_specs=[ANY] * 2 + [HBM] * (2 * n),
        out_specs=[ANY] * n,
        scratch_shapes=[
            pltpu.VMEM((m, width), BF16),
            pltpu.VMEM((2 * n * rows, width), BF16),
            pltpu.VMEM((n, m, depth), BF16),
            pltpu.SemaphoreType.DMA((2 + 2 * n,)),
            pltpu.SemaphoreType.DMA((n,)),
        ],
        compiler_params=params(32 << 20),
        cost_estimate=pl.CostEstimate(flops=1, bytes_accessed=1, transcendentals=0),
        name="back",
    )(keep, came, *own, *other)
    return list(outs)


def pick_kernel(bits, *refs):
    n = 1 << bits
    blocks, outs, (room, sems) = refs[:n], refs[n : 2 * n], refs[2 * n :]
    _, base = where_am_i(bits)
    for copy in copy_all([(blocks[l], room.at[l]) for l in range(n)], sems):
        copy.wait()
    for copy in copy_all([(room.at[base ^ j], outs[j]) for j in range(n)], sems):
        copy.wait()


def pick(blocks, bits):
    n = len(blocks)
    return pl.pallas_call(
        functools.partial(pick_kernel, bits),
        out_shape=[jax.ShapeDtypeStruct(blocks[0].shape, BF16)] * n,
        in_specs=[HBM] * n,
        out_specs=[ANY] * n,
        scratch_shapes=[pltpu.VMEM((n, *blocks[0].shape), BF16), pltpu.SemaphoreType.DMA((n,))],
        compiler_params=params(16 << 20),
        cost_estimate=pl.CostEstimate(flops=1, bytes_accessed=1, transcendentals=0),
        name="pick",
    )(*blocks)


def total(parts):
    return sum(part.astype(F32) for part in parts).astype(BF16)


def after(value, *others):
    return lax.optimization_barrier((value, *others))[0]


def per_device(rows, cols, amplitudes, factor, kernel):
    chips = rows // 2
    bits = chips.bit_length() - 1
    core = lax.rem(lax.axis_index("row"), 2)

    def distance(row, mask):
        return mask if row % 2 == 0 else flipped(mask, bits)

    def swap(value):
        return lax.ppermute(value, "row", [(r, r ^ 1) for r in range(rows)])

    def in_plane(mask):
        return lambda value: lax.ppermute(value, "row", [(r, r ^ (2 * distance(r, mask))) for r in range(rows)])

    def in_line(mask):
        pairs = [(r * cols + c, r * cols + (c ^ distance(r, mask))) for r in range(rows) for c in range(cols)]
        return lambda value: lax.ppermute(value, ("row", "col"), pairs)

    plane = [in_plane(1 << t) for t in range(bits)]
    line = [in_line(1 << t) for t in range(bits)]

    def gather(block, sends, gates=(), chained=False):
        blocks = [block]
        for t, send in enumerate(sends):
            first = after(block, *gates[t]) if t < len(gates) else block
            fresh = [send(first)]
            blocks = blocks + fresh + [send(after(b, *fresh) if chained else b) for b in blocks[1:]]
        return blocks

    def scatter(blocks, sends, gates=None):
        parts, marks = [], None
        for t in range(len(sends) - 1, -1, -1):
            n = 1 << t
            away = blocks[n:]
            if gates is not None and marks is None:
                away = [after(block, *gates) for block in away]
            got = [sends[t](block) for block in away]
            marks = got if marks is None else marks
            parts.append(got[0])
            blocks = [blocks[0]] + [total([blocks[j], got[j]]) for j in range(1, n)]
        return [blocks[0], *parts], marks

    def column_halves(value):
        half = value.shape[1] // 2
        return [lax.dynamic_slice_in_dim(value, which * half, half, 1) for which in (core, 1 - core)]

    line_own = gather(factor, line, chained=True)
    cols_own = gather(factor, plane)
    kernel_own, kernel_away = column_halves(kernel)
    kernel_other = swap(kernel_away)
    cols_other = [swap(b) for b in cols_own]
    terms = [gather(amplitudes[0], line, [[line_own[-1]]] * bits)]
    terms.append(gather(amplitudes[1], line, [[terms[0][1]]] + [[terms[0][-1]]] * (bits - 1)))

    pieces = pick(line_own, bits)
    first_own = [pieces[0]] + [in_plane(j)(pieces[j]) for j in range(1, chips)]
    first_other = [swap(b) for b in first_own]

    gates, results, marks = first_own[1:], [], [None, None]
    for pair in range(amplitudes.shape[0]):
        keep, away = project(terms[pair], cols_own, cols_other, bits)
        block = jnp.concatenate([keep, swap(away)])
        proj = gather(block, plane, [gates] * bits)
        gates = proj[1:3]
        backs = grid(proj, first_own, first_other, kernel_own, kernel_other, bits)
        parts, marks[0] = scatter(backs, plane, marks[0])
        rest = amplitudes.shape[1]
        came = swap(total([part[rest:] for part in parts]))
        keep = total([part[:rest] for part in parts])
        outs = back(keep, came, cols_own, cols_other, bits)
        parts, marks[1] = scatter(outs, line, marks[1])
        results.append(total(parts))
    return jnp.stack(results)


def solution(mesh):
    placed = (P(None, "row", "col"), P("row", "col"), P("row", "col"))
    rows, cols = mesh.shape["row"], mesh.shape["col"]
    return jax.shard_map(
        functools.partial(per_device, rows, cols), mesh=mesh, in_specs=placed, out_specs=P(None, "row", "col"), check_vma=False
    )
```

```python
import functools

import jax
import jax.numpy as jnp
from jax import lax
from jax.experimental import pallas as pl
from jax.experimental.pallas import tpu as pltpu
from jax.sharding import PartitionSpec as P

BF16 = jnp.bfloat16
F32 = jnp.float32
ANY = pl.BlockSpec(memory_space=pl.ANY)
HBM = pl.BlockSpec(memory_space=pltpu.HBM)


def flipped(value, bits):
    total = 0
    for t in range(bits):
        total = total + (((value >> t) & 1) << (bits - 1 - t))
    return total


def params(vmem):
    return pltpu.CompilerParams(vmem_limit_bytes=vmem)


def where_am_i(bits):
    row, col = lax.axis_index("row"), lax.axis_index("col")
    core, chip = lax.rem(row, 2), row // 2
    offset = chip ^ col
    base = jnp.where(core == 0, offset, flipped(offset, bits))
    return core, base


def copy_all(pairs, sems):
    copies = [pltpu.make_async_copy(a, b, sems.at[s]) for s, (a, b) in enumerate(pairs)]
    for copy in copies:
        copy.start()
    return copies


def plane_pairs(own, other, room, core, rows, bits):
    pairs = []
    for j, ref in enumerate(own):
        pairs.append((ref, room.at[pl.ds((2 * j + core) * rows, rows)]))
    for j, ref in enumerate(other):
        pairs.append((ref, room.at[pl.ds((2 * flipped(j, bits) + 1 - core) * rows, rows)]))
    return pairs


def halves(ref, core):
    half = ref.shape[1] // 2
    return [ref.at[:, pl.ds(pl.multiple_of(which * half, half), half)] for which in (core, 1 - core)]


def project_kernel(bits, *refs):
    n = 1 << bits
    terms, own, other = refs[:n], refs[n : 2 * n], refs[2 * n : 3 * n]
    keep, away, held, room, result, sems = refs[3 * n :]
    core, base = where_am_i(bits)
    rows, width = own[0].shape
    depth = terms[0].shape[1]
    loads = copy_all([(terms[l], held.at[l]) for l in range(n)] + plane_pairs(own, other, room, core, rows, bits), sems)
    for copy in loads[:n]:
        copy.wait()
    acc = jnp.zeros((rows, width), F32)
    for j in range(n):
        loads[n + j].wait()
        loads[2 * n + flipped(j, bits)].wait()
        acc = acc + jnp.dot(held[base ^ j], room[pl.ds(j * depth, depth), :], preferred_element_type=F32)
    result[...] = acc.astype(BF16)

    for copy in copy_all(list(zip(halves(result, core), (keep, away))), sems):
        copy.wait()


def project(terms, own, other, bits):
    n = len(terms)
    m, depth = terms[0].shape
    rows, width = own[0].shape
    return pl.pallas_call(
        functools.partial(project_kernel, bits),
        out_shape=[jax.ShapeDtypeStruct((m, width // 2), BF16)] * 2,
        in_specs=[HBM] * (3 * n),
        out_specs=[ANY] * 2,
        scratch_shapes=[
            pltpu.VMEM((n, m, depth), BF16),
            pltpu.VMEM((2 * n * rows, width), BF16),
            pltpu.VMEM((m, width), BF16),
            pltpu.SemaphoreType.DMA((3 * n,)),
        ],
        compiler_params=params(32 << 20),
        cost_estimate=pl.CostEstimate(flops=1, bytes_accessed=1, transcendentals=0),
        name="project",
    )(*terms, *own, *other)


def grid_kernel(bits, *refs):
    n = 1 << bits
    proj_in, own, other = refs[:n], refs[n : 2 * n], refs[2 * n : 3 * n]
    kernel_own, kernel_other = refs[3 * n : 3 * n + 2]
    outs = refs[3 * n + 2 : 4 * n + 2]
    proj, room, coulomb, total_ref, scaled, result, sems, tile_sems, out_sems = refs[4 * n + 2 :]
    core, _ = where_am_i(bits)
    rows = own[0].shape[0]
    half = kernel_own.shape[0]
    pairs = []
    for j in range(n):
        pairs.append((own[j], room.at[pl.ds(2 * j * rows, rows)]))
        pairs.append((other[flipped(j, bits)], room.at[pl.ds((2 * j + 1) * rows, rows)]))
        pairs.append((proj_in[j], proj.at[pl.ds(2 * j * rows, 2 * rows)]))
    loads = copy_all(pairs, sems)
    late = copy_all([(kernel_own, coulomb.at[pl.ds(core * half, half)]), (kernel_other, coulomb.at[pl.ds((1 - core) * half, half)])], tile_sems)
    for j in range(n):
        at = pl.ds(2 * j * rows, 2 * rows)
        for copy in loads[3 * j : 3 * j + 3]:
            copy.wait()
        term = lax.dot_general(room[at, :], proj[at, :], (((0,), (0,)), ((), ())), preferred_element_type=F32)
        total_ref[...] = term if j == 0 else total_ref[...] + term
    for copy in late:
        copy.wait()
    scaled[...] = (coulomb[...] * total_ref[...]).astype(BF16)

    copies = []
    for j in range(n - 1, -1, -1):
        at = pl.ds(2 * j * rows, 2 * rows)
        result[at, :] = jnp.dot(room[at, :], scaled[...], preferred_element_type=F32).astype(BF16)
        copy = pltpu.make_async_copy(result.at[at], outs[j], out_sems.at[j])
        copy.start()
        copies.append(copy)
    for copy in copies:
        copy.wait()


def grid(proj, own, other, kernel_own, kernel_other, bits):
    n = len(proj)
    rows, width = own[0].shape
    cols = proj[0].shape[1]
    outs = pl.pallas_call(
        functools.partial(grid_kernel, bits),
        out_shape=[jax.ShapeDtypeStruct((2 * rows, cols), BF16)] * n,
        in_specs=[HBM] * (3 * n) + [ANY] * 2,
        out_specs=[ANY] * n,
        scratch_shapes=[
            pltpu.VMEM((2 * n * rows, cols), BF16),
            pltpu.VMEM((2 * n * rows, width), BF16),
            pltpu.VMEM((width, cols), F32),
            pltpu.VMEM((width, cols), F32),
            pltpu.VMEM((width, cols), BF16),
            pltpu.VMEM((2 * n * rows, cols), BF16),
            pltpu.SemaphoreType.DMA((3 * n,)),
            pltpu.SemaphoreType.DMA((2,)),
            pltpu.SemaphoreType.DMA((n,)),
        ],
        compiler_params=params(40 << 20),
        cost_estimate=pl.CostEstimate(flops=1, bytes_accessed=1, transcendentals=0),
        name="grid",
    )(*proj, *own, *other, kernel_own, kernel_other)
    return list(outs)


def back_kernel(bits, *refs):
    n = 1 << bits
    keep, came, own, other = refs[0], refs[1], refs[2 : 2 + n], refs[2 + n : 2 + 2 * n]
    outs = refs[2 + 2 * n : 2 + 3 * n]
    given, room, results, sems, out_sems = refs[2 + 3 * n :]
    core, base = where_am_i(bits)
    rows, width = own[0].shape
    depth = outs[0].shape[1]
    pairs = plane_pairs(own, other, room, core, rows, bits) + list(zip((keep, came), halves(given, core)))
    for copy in copy_all(pairs, sems):
        copy.wait()
    copies = []
    for l in range(n - 1, -1, -1):
        right = room[pl.ds(pl.multiple_of((base ^ l) * depth, depth), depth), :]
        results[l] = lax.dot_general(given[...], right, (((1,), (1,)), ((), ())), preferred_element_type=F32).astype(BF16)
        copy = pltpu.make_async_copy(results.at[l], outs[l], out_sems.at[l])
        copy.start()
        copies.append(copy)
    for copy in copies:
        copy.wait()


def back(keep, came, own, other, bits):
    n = len(own)
    rows, width = own[0].shape
    m, depth = keep.shape[0], 2 * rows
    outs = pl.pallas_call(
        functools.partial(back_kernel, bits),
        out_shape=[jax.ShapeDtypeStruct((m, depth), BF16)] * n,
        in_specs=[ANY] * 2 + [HBM] * (2 * n),
        out_specs=[ANY] * n,
        scratch_shapes=[
            pltpu.VMEM((m, width), BF16),
            pltpu.VMEM((2 * n * rows, width), BF16),
            pltpu.VMEM((n, m, depth), BF16),
            pltpu.SemaphoreType.DMA((2 + 2 * n,)),
            pltpu.SemaphoreType.DMA((n,)),
        ],
        compiler_params=params(32 << 20),
        cost_estimate=pl.CostEstimate(flops=1, bytes_accessed=1, transcendentals=0),
        name="back",
    )(keep, came, *own, *other)
    return list(outs)


def pick_kernel(bits, *refs):
    n = 1 << bits
    blocks, outs, (room, sems) = refs[:n], refs[n : 2 * n], refs[2 * n :]
    _, base = where_am_i(bits)
    for copy in copy_all([(blocks[l], room.at[l]) for l in range(n)], sems):
        copy.wait()
    for copy in copy_all([(room.at[base ^ j], outs[j]) for j in range(n)], sems):
        copy.wait()


def pick(blocks, bits):
    n = len(blocks)
    return pl.pallas_call(
        functools.partial(pick_kernel, bits),
        out_shape=[jax.ShapeDtypeStruct(blocks[0].shape, BF16)] * n,
        in_specs=[HBM] * n,
        out_specs=[ANY] * n,
        scratch_shapes=[pltpu.VMEM((n, *blocks[0].shape), BF16), pltpu.SemaphoreType.DMA((n,))],
        compiler_params=params(16 << 20),
        cost_estimate=pl.CostEstimate(flops=1, bytes_accessed=1, transcendentals=0),
        name="pick",
    )(*blocks)


def total(parts):
    return sum(part.astype(F32) for part in parts).astype(BF16)


def after(value, *others):
    return lax.optimization_barrier((value, *others))[0]


def per_device(rows, cols, amplitudes, factor, kernel):
    chips = rows // 2
    bits = chips.bit_length() - 1
    core = lax.rem(lax.axis_index("row"), 2)

    def distance(row, mask):
        return mask if row % 2 == 0 else flipped(mask, bits)

    def swap(value):
        return lax.ppermute(value, "row", [(r, r ^ 1) for r in range(rows)])

    def in_plane(mask):
        return lambda value: lax.ppermute(value, "row", [(r, r ^ (2 * distance(r, mask))) for r in range(rows)])

    def in_line(mask):
        pairs = [(r * cols + c, r * cols + (c ^ distance(r, mask))) for r in range(rows) for c in range(cols)]
        return lambda value: lax.ppermute(value, ("row", "col"), pairs)

    plane = [in_plane(1 << t) for t in range(bits)]
    line = [in_line(1 << t) for t in range(bits)]

    def gather(block, sends, gates=(), chained=False):
        blocks = [block]
        for t, send in enumerate(sends):
            first = after(block, *gates[t]) if t < len(gates) else block
            fresh = [send(first)]
            blocks = blocks + fresh + [send(after(b, *fresh) if chained else b) for b in blocks[1:]]
        return blocks

    def scatter(blocks, sends, gates=None):
        parts, marks = [], None
        for t in range(len(sends) - 1, -1, -1):
            n = 1 << t
            away = blocks[n:]
            if gates is not None and marks is None:
                away = [after(block, *gates[:1]) for j, block in enumerate(away)]
            got = [sends[t](block) for block in away]
            marks = got if marks is None else marks
            parts.append(got[0])
            blocks = [blocks[0]] + [total([blocks[j], got[j]]) for j in range(1, n)]
        return [blocks[0], *parts], marks

    def column_halves(value):
        half = value.shape[1] // 2
        return [lax.dynamic_slice_in_dim(value, which * half, half, 1) for which in (core, 1 - core)]

    line_own = gather(factor, line, chained=True)
    cols_own = gather(factor, plane)
    kernel_own, kernel_away = column_halves(kernel)
    kernel_other = swap(kernel_away)
    cols_other = [swap(b) for b in cols_own]
    terms = [gather(amplitudes[0], line, [[line_own[-1]]] * bits)]
    terms.append(gather(amplitudes[1], line, [[terms[0][1]]] * bits))

    pieces = pick(line_own, bits)
    first_own = [pieces[0]] + [in_plane(j)(pieces[j]) for j in range(1, chips)]
    first_other = [swap(b) for b in first_own]

    gates, results, marks, outs = first_own[1:], [], [None, None], ()
    for pair in range(amplitudes.shape[0]):
        keep, away = project(terms[pair], cols_own, cols_other, bits)
        block = jnp.concatenate([keep, swap(away)])
        proj = gather(block, plane, [gates] * bits)
        gates = proj[1:3]
        backs = grid(proj, first_own, first_other, kernel_own, kernel_other, bits)
        parts, marks[0] = scatter(backs, plane, marks[0])
        parts = [after(part, *outs) if outs else part for part in parts]
        rest = amplitudes.shape[1]
        came = swap(total([part[rest:] for part in parts]))
        keep = total([part[:rest] for part in parts])
        outs = back(keep, came, cols_own, cols_other, bits)
        parts, marks[1] = scatter(outs, line, marks[1])
        results.append(total(parts))
    return jnp.stack(results)


def solution(mesh):
    placed = (P(None, "row", "col"), P("row", "col"), P("row", "col"))
    rows, cols = mesh.shape["row"], mesh.shape["col"]
    return jax.shard_map(
        functools.partial(per_device, rows, cols), mesh=mesh, in_specs=placed, out_specs=P(None, "row", "col"), check_vma=False
    )
```

```python
import functools

import jax
import jax.numpy as jnp
from jax import lax
from jax.experimental import pallas as pl
from jax.experimental.pallas import tpu as pltpu
from jax.sharding import PartitionSpec as P

BF16 = jnp.bfloat16
F32 = jnp.float32
ANY = pl.BlockSpec(memory_space=pl.ANY)
HBM = pl.BlockSpec(memory_space=pltpu.HBM)


def flipped(value, bits):
    total = 0
    for t in range(bits):
        total = total + (((value >> t) & 1) << (bits - 1 - t))
    return total


def params(vmem):
    return pltpu.CompilerParams(vmem_limit_bytes=vmem)


def where_am_i(bits):
    row, col = lax.axis_index("row"), lax.axis_index("col")
    core, chip = lax.rem(row, 2), row // 2
    offset = chip ^ col
    base = jnp.where(core == 0, offset, flipped(offset, bits))
    return core, base


def copy_all(pairs, sems):
    copies = [pltpu.make_async_copy(a, b, sems.at[s]) for s, (a, b) in enumerate(pairs)]
    for copy in copies:
        copy.start()
    return copies


def plane_pairs(own, other, room, core, rows, bits):
    pairs = []
    for j, ref in enumerate(own):
        pairs.append((ref, room.at[pl.ds((2 * j + core) * rows, rows)]))
    for j, ref in enumerate(other):
        pairs.append((ref, room.at[pl.ds((2 * flipped(j, bits) + 1 - core) * rows, rows)]))
    return pairs


def halves(ref, core):
    half = ref.shape[1] // 2
    return [ref.at[:, pl.ds(pl.multiple_of(which * half, half), half)] for which in (core, 1 - core)]


def project_kernel(bits, *refs):
    n = 1 << bits
    terms, own, other = refs[:n], refs[n : 2 * n], refs[2 * n : 3 * n]
    keep, away, held, room, result, sems = refs[3 * n :]
    core, base = where_am_i(bits)
    rows, width = own[0].shape
    depth = terms[0].shape[1]
    loads = copy_all([(terms[l], held.at[l]) for l in range(n)] + plane_pairs(own, other, room, core, rows, bits), sems)
    for copy in loads[:n]:
        copy.wait()
    acc = jnp.zeros((rows, width), F32)
    for j in range(n):
        loads[n + j].wait()
        loads[2 * n + flipped(j, bits)].wait()
        acc = acc + jnp.dot(held[base ^ j], room[pl.ds(j * depth, depth), :], preferred_element_type=F32)
    result[...] = acc.astype(BF16)

    for copy in copy_all(list(zip(halves(result, core), (keep, away))), sems):
        copy.wait()


def project(terms, own, other, bits):
    n = len(terms)
    m, depth = terms[0].shape
    rows, width = own[0].shape
    return pl.pallas_call(
        functools.partial(project_kernel, bits),
        out_shape=[jax.ShapeDtypeStruct((m, width // 2), BF16)] * 2,
        in_specs=[HBM] * (3 * n),
        out_specs=[ANY] * 2,
        scratch_shapes=[
            pltpu.VMEM((n, m, depth), BF16),
            pltpu.VMEM((2 * n * rows, width), BF16),
            pltpu.VMEM((m, width), BF16),
            pltpu.SemaphoreType.DMA((3 * n,)),
        ],
        compiler_params=params(32 << 20),
        cost_estimate=pl.CostEstimate(flops=1, bytes_accessed=1, transcendentals=0),
        name="project",
    )(*terms, *own, *other)


def grid_kernel(bits, *refs):
    n = 1 << bits
    proj_in, own, other = refs[:n], refs[n : 2 * n], refs[2 * n : 3 * n]
    kernel_own, kernel_other = refs[3 * n : 3 * n + 2]
    outs = refs[3 * n + 2 : 4 * n + 2]
    proj, room, coulomb, total_ref, scaled, result, sems, tile_sems, out_sems = refs[4 * n + 2 :]
    core, _ = where_am_i(bits)
    rows = own[0].shape[0]
    half = kernel_own.shape[0]
    pairs = []
    for j in range(n):
        pairs.append((own[j], room.at[pl.ds(2 * j * rows, rows)]))
        pairs.append((other[flipped(j, bits)], room.at[pl.ds((2 * j + 1) * rows, rows)]))
        pairs.append((proj_in[j], proj.at[pl.ds(2 * j * rows, 2 * rows)]))
    loads = copy_all(pairs, sems)
    late = copy_all([(kernel_own, coulomb.at[pl.ds(core * half, half)]), (kernel_other, coulomb.at[pl.ds((1 - core) * half, half)])], tile_sems)
    for j in range(n):
        at = pl.ds(2 * j * rows, 2 * rows)
        for copy in loads[3 * j : 3 * j + 3]:
            copy.wait()
        term = lax.dot_general(room[at, :], proj[at, :], (((0,), (0,)), ((), ())), preferred_element_type=F32)
        total_ref[...] = term if j == 0 else total_ref[...] + term
    for copy in late:
        copy.wait()
    scaled[...] = (coulomb[...] * total_ref[...]).astype(BF16)

    copies = []
    for j in range(n - 1, -1, -1):
        at = pl.ds(2 * j * rows, 2 * rows)
        result[at, :] = jnp.dot(room[at, :], scaled[...], preferred_element_type=F32).astype(BF16)
        copy = pltpu.make_async_copy(result.at[at], outs[j], out_sems.at[j])
        copy.start()
        copies.append(copy)
    for copy in copies:
        copy.wait()


def grid(proj, own, other, kernel_own, kernel_other, bits):
    n = len(proj)
    rows, width = own[0].shape
    cols = proj[0].shape[1]
    outs = pl.pallas_call(
        functools.partial(grid_kernel, bits),
        out_shape=[jax.ShapeDtypeStruct((2 * rows, cols), BF16)] * n,
        in_specs=[HBM] * (3 * n) + [ANY] * 2,
        out_specs=[ANY] * n,
        scratch_shapes=[
            pltpu.VMEM((2 * n * rows, cols), BF16),
            pltpu.VMEM((2 * n * rows, width), BF16),
            pltpu.VMEM((width, cols), F32),
            pltpu.VMEM((width, cols), F32),
            pltpu.VMEM((width, cols), BF16),
            pltpu.VMEM((2 * n * rows, cols), BF16),
            pltpu.SemaphoreType.DMA((3 * n,)),
            pltpu.SemaphoreType.DMA((2,)),
            pltpu.SemaphoreType.DMA((n,)),
        ],
        compiler_params=params(40 << 20),
        cost_estimate=pl.CostEstimate(flops=1, bytes_accessed=1, transcendentals=0),
        name="grid",
    )(*proj, *own, *other, kernel_own, kernel_other)
    return list(outs)


def back_kernel(bits, *refs):
    n = 1 << bits
    keep, came, own, other = refs[0], refs[1], refs[2 : 2 + n], refs[2 + n : 2 + 2 * n]
    outs = refs[2 + 2 * n : 2 + 3 * n]
    given, room, results, sems, out_sems = refs[2 + 3 * n :]
    core, base = where_am_i(bits)
    rows, width = own[0].shape
    depth = outs[0].shape[1]
    loads = copy_all(list(zip((keep, came), halves(given, core))) + plane_pairs(own, other, room, core, rows, bits), sems)
    for copy in loads[:2]:
        copy.wait()
    for j in range(n):
        loads[2 + j].wait()
        loads[2 + n + flipped(j, bits)].wait()
        right = room[pl.ds(j * depth, depth), :]
        results[base ^ j] = lax.dot_general(given[...], right, (((1,), (1,)), ((), ())), preferred_element_type=F32).astype(BF16)
    for copy in copy_all([(results.at[l], outs[l]) for l in range(n)], out_sems):
        copy.wait()


def back(keep, came, own, other, bits):
    n = len(own)
    rows, width = own[0].shape
    m, depth = keep.shape[0], 2 * rows
    outs = pl.pallas_call(
        functools.partial(back_kernel, bits),
        out_shape=[jax.ShapeDtypeStruct((m, depth), BF16)] * n,
        in_specs=[ANY] * 2 + [HBM] * (2 * n),
        out_specs=[ANY] * n,
        scratch_shapes=[
            pltpu.VMEM((m, width), BF16),
            pltpu.VMEM((2 * n * rows, width), BF16),
            pltpu.VMEM((n, m, depth), BF16),
            pltpu.SemaphoreType.DMA((2 + 2 * n,)),
            pltpu.SemaphoreType.DMA((n,)),
        ],
        compiler_params=params(32 << 20),
        cost_estimate=pl.CostEstimate(flops=1, bytes_accessed=1, transcendentals=0),
        name="back",
    )(keep, came, *own, *other)
    return list(outs)


def pick_kernel(bits, *refs):
    n = 1 << bits
    blocks, outs, (room, sems) = refs[:n], refs[n : 2 * n], refs[2 * n :]
    _, base = where_am_i(bits)
    for copy in copy_all([(blocks[l], room.at[l]) for l in range(n)], sems):
        copy.wait()
    for copy in copy_all([(room.at[base ^ j], outs[j]) for j in range(n)], sems):
        copy.wait()


def pick(blocks, bits):
    n = len(blocks)
    return pl.pallas_call(
        functools.partial(pick_kernel, bits),
        out_shape=[jax.ShapeDtypeStruct(blocks[0].shape, BF16)] * n,
        in_specs=[HBM] * n,
        out_specs=[ANY] * n,
        scratch_shapes=[pltpu.VMEM((n, *blocks[0].shape), BF16), pltpu.SemaphoreType.DMA((n,))],
        compiler_params=params(16 << 20),
        cost_estimate=pl.CostEstimate(flops=1, bytes_accessed=1, transcendentals=0),
        name="pick",
    )(*blocks)


def total(parts):
    return sum(part.astype(F32) for part in parts).astype(BF16)


def after(value, *others):
    return lax.optimization_barrier((value, *others))[0]


def per_device(rows, cols, amplitudes, factor, kernel):
    chips = rows // 2
    bits = chips.bit_length() - 1
    core = lax.rem(lax.axis_index("row"), 2)

    def distance(row, mask):
        return mask if row % 2 == 0 else flipped(mask, bits)

    def swap(value):
        return lax.ppermute(value, "row", [(r, r ^ 1) for r in range(rows)])

    def in_plane(mask):
        return lambda value: lax.ppermute(value, "row", [(r, r ^ (2 * distance(r, mask))) for r in range(rows)])

    def in_line(mask):
        pairs = [(r * cols + c, r * cols + (c ^ distance(r, mask))) for r in range(rows) for c in range(cols)]
        return lambda value: lax.ppermute(value, ("row", "col"), pairs)

    plane = [in_plane(1 << t) for t in range(bits)]
    line = [in_line(1 << t) for t in range(bits)]

    def gather(block, sends, gates=(), chained=False):
        blocks = [block]
        for t, send in enumerate(sends):
            first = after(block, *gates[t]) if t < len(gates) else block
            fresh = [send(first)]
            blocks = blocks + fresh + [send(after(b, *fresh) if chained else b) for b in blocks[1:]]
        return blocks

    def scatter(blocks, sends, gates=None):
        parts, marks = [], None
        for t in range(len(sends) - 1, -1, -1):
            n = 1 << t
            away = blocks[n:]
            if gates is not None and marks is None:
                away = [after(block, *gates[:1]) for j, block in enumerate(away)]
            got = [sends[t](block) for block in away]
            marks = got if marks is None else marks
            parts.append(got[0])
            blocks = [blocks[0]] + [total([blocks[j], got[j]]) for j in range(1, n)]
        return [blocks[0], *parts], marks

    def column_halves(value):
        half = value.shape[1] // 2
        return [lax.dynamic_slice_in_dim(value, which * half, half, 1) for which in (core, 1 - core)]

    line_own = gather(factor, line, chained=True)
    cols_own = gather(factor, plane)
    kernel_own, kernel_away = column_halves(kernel)
    kernel_other = swap(after(kernel_away, line_own[1]))
    cols_other = [swap(b) for b in cols_own]
    terms = [gather(amplitudes[0], line, [[line_own[-1]]] * bits)]
    terms.append(gather(amplitudes[1], line, [[terms[0][1]]] * bits))

    pieces = pick(line_own, bits)
    first_own = [pieces[0]] + [in_plane(j)(pieces[j]) for j in range(1, chips)]
    first_other = [swap(after(b, terms[1][-1])) for b in first_own]

    gates, results, marks, outs = first_own[1:], [], [None, None], ()
    for pair in range(amplitudes.shape[0]):
        keep, away = project(terms[pair], cols_own, cols_other, bits)
        block = jnp.concatenate([keep, swap(away)])
        proj = gather(block, plane, [gates] * bits)
        gates = proj[1:3]
        backs = grid(proj, first_own, first_other, kernel_own, kernel_other, bits)
        parts, marks[0] = scatter(backs, plane, marks[0])
        parts = [after(part, *outs) if outs else part for part in parts]
        rest = amplitudes.shape[1]
        came = swap(total([part[rest:] for part in parts]))
        keep = total([part[:rest] for part in parts])
        outs = back(keep, came, cols_own, cols_other, bits)
        parts, marks[1] = scatter(outs, line, marks[1])
        results.append(total(parts))
    return jnp.stack(results)


def solution(mesh):
    placed = (P(None, "row", "col"), P("row", "col"), P("row", "col"))
    rows, cols = mesh.shape["row"], mesh.shape["col"]
    return jax.shard_map(
        functools.partial(per_device, rows, cols), mesh=mesh, in_specs=placed, out_specs=P(None, "row", "col"), check_vma=False
    )
```
